1024 devices in a mesh: owner: 32 (over z), slab: 4 (over y), red: 8 (over x, core).
Axes of the slice: x: 4, y: 4, z: 32, core: 2. Of those that a mesh axis runs over, the one named last changes fastest.
Arguments:
- amplitudes: bfloat16 [2048, 128, 256], P(('owner', 'slab', 'red')), may hold values from -6 to 6
- integrals: bfloat16 [64, 128, 128], P('slab'), may hold values from -0.21875 to 0.21875
- requests: int32 [32, 4, 8, 32], P('owner', 'slab', 'red'), may hold values from 0 to 1
- task_slot: int32 [32, 4, 8, 16, 12], P('owner', 'slab', 'red'), may hold values from 0 to 31
- task_integral: int32 [32, 4, 8, 16, 12], P('owner', 'slab', 'red'), may hold values from 0 to 63
- live_tasks: int32 [32, 4, 8], P('owner', 'slab', 'red'), may hold values from 3 to 12, as said below
- denominators: float32 [2048, 128, 256], P(('owner', 'slab', 'red')), may hold values from 0.5 to 5
Outputs:
- update: float32 [2048, 128, 256], P(('owner', 'slab', 'red'))
The draws below stay inside these ranges and needn't reach their ends.
Inputs may be any that keep to these rules, and one draw needn't show every extreme that they name: `live_tasks`: slots below a device's count are live; in every draw some devices have all 12 live.
All inputs are finite; a program needn't handle non-finite values.
Results may differ from the reference program's by a relative error of at most 0.0003.
Values may be sent and summed in bfloat16 or wider, within the bound.
No kernel may reach another device: no remote copies, remote signals or barrier semaphores. Data moves between devices by JAX's collectives and lax.ppermute only.
A program may use at most 32 MiB of HBM per device.

```python
import math
import jax
import jax.numpy as jnp
from jax import lax

TILE = 128
COLUMNS = 256
OWNED = 2
SLOTS = 12
AMP_TILES = 2048
INT_TILES = 64
GROUP_OUT = 16
OUT_TOTAL = 2048
N_OWNER = 32
N_SLAB = 4
N_RED = 8


def draw_live_tasks(key, part):
    base_key = jax.random.fold_in(key, 7)
    first_key, second_key = jax.random.split(base_key)
    devices_all = N_OWNER * N_SLAB * N_RED
    base = jax.random.randint(first_key, (devices_all,), SLOTS // 4, SLOTS // 2 + 1, dtype=jnp.int32)
    order = jax.random.permutation(second_key, devices_all)
    heavy = order < max(devices_all // 16, 1)
    filled = jnp.where(heavy, SLOTS, base).astype(jnp.int32)
    return filled.reshape(N_OWNER, N_SLAB, N_RED)


def touch_ends(values, stream_key, low, top_value):
    extent = values.shape
    index_at = [jax.random.randint(jax.random.fold_in(stream_key, axis), (), 0, extent[axis]) for axis in range(len(extent))]
    values = values.at[tuple(index_at)].set(low)
    longest = extent.index(max(extent))
    index_at[longest] = (index_at[longest] + 1) % extent[longest]
    return values.at[tuple(index_at)].set(top_value)


def level_of(key, extent, cuts, low, high):
    def one(dim, parts):
        steps = jax.random.uniform(jax.random.fold_in(jax.random.fold_in(key, 6), dim), (parts,), jnp.float32, low / len(cuts), high / len(cuts))
        return jnp.repeat(jnp.exp(steps), extent[dim] // parts).reshape((-1,) + (1,) * (len(extent) - dim - 1))

    factor_of = one(*cuts[0])
    for cut in cuts[1:]:
        factor_of = factor_of * one(*cut)
    return factor_of


def gaussian(own_key, shape, scale, bound, cuts=(), kind=jnp.bfloat16):
    drawn = jax.random.normal(own_key, shape, jnp.float32) * scale
    if len(cuts) > 0:
        drawn = level_of(own_key, shape, cuts, -0.22, 0.18) * drawn
    return jnp.clip(drawn, min=-bound, max=bound).astype(kind)


def setup_inputs(seed: int = 0) -> dict:
    arg_keys = jax.random.split(jax.random.key(seed), 8)
    return {
        "amplitudes": gaussian(arg_keys[0], (AMP_TILES, TILE, COLUMNS), 1.0, 6.0, ((0, 1024),)),
        "integrals": gaussian(arg_keys[1], (INT_TILES, TILE, TILE), (TILE * SLOTS // 2) ** -0.5, 0.21875, ((0, 4),)),
        "requests": touch_ends(jax.random.randint(arg_keys[2], (N_OWNER, N_SLAB, N_RED, N_OWNER), 0, OWNED), jax.random.fold_in(arg_keys[2], 1), 0, OWNED - 1).astype(jnp.int32),
        "task_slot": touch_ends(jax.random.randint(arg_keys[3], (N_OWNER, N_SLAB, N_RED, GROUP_OUT, SLOTS), 0, N_OWNER), jax.random.fold_in(arg_keys[3], 1), 0, N_OWNER - 1).astype(jnp.int32),
        "task_integral": touch_ends(jax.random.randint(arg_keys[4], (N_OWNER, N_SLAB, N_RED, GROUP_OUT, SLOTS), 0, INT_TILES), jax.random.fold_in(arg_keys[4], 1), 0, INT_TILES - 1).astype(jnp.int32),
        "live_tasks": draw_live_tasks(jax.random.fold_in(arg_keys[7], 71), 0),
        "denominators": jnp.clip(jnp.exp(math.log(5.0) - 2.3025851 * jax.random.uniform(arg_keys[6], (OUT_TOTAL, TILE, COLUMNS), jnp.float32) ** level_of(arg_keys[6], (OUT_TOTAL, TILE, COLUMNS), ((0, 1024),), -0.2, 0.2)), 0.5, 5.0),
    }


def device_partial(column_tiles, integrals, wanted, slot_table, integral_table, live_count):
    pulled = column_tiles[jnp.arange(N_OWNER, dtype=jnp.int32), wanted.astype(jnp.int32)]
    live_mask = (jnp.arange(SLOTS, dtype=jnp.int32) < live_count).astype(jnp.float32)
    integral_rows = integrals[integral_table].astype(jnp.float32) * live_mask[None, :, None, None]
    amplitude_rows = pulled[slot_table].astype(jnp.float32)
    return jnp.einsum("qkac,qkcx->qax", integral_rows, amplitude_rows, precision=lax.Precision.HIGHEST)


def reference(amplitudes, integrals, requests, task_slot, task_integral, live_tasks, denominators):
    groups = N_OWNER * N_SLAB
    blocks = amplitudes.reshape(N_OWNER, N_SLAB, N_RED, OWNED, TILE, COLUMNS)
    per_column = jnp.transpose(blocks, (1, 2, 0, 3, 4, 5))
    request_rows = requests.reshape(groups, N_RED, N_OWNER)
    slot_rows = task_slot.reshape(groups, N_RED, GROUP_OUT, SLOTS)
    integral_ids = task_integral.reshape(groups, N_RED, GROUP_OUT, SLOTS)
    live_rows = live_tasks.reshape(groups, N_RED)
    slab_ids = jnp.tile(jnp.arange(N_SLAB, dtype=jnp.int32), N_OWNER)
    red_ids = jnp.arange(N_RED, dtype=jnp.int32)

    def one_group(bundle):
        slab_index, wanted_rows, slot_group, integral_group, live_group = bundle

        def add_member(summed, member):
            red_index, wanted, slot_table, integral_table, live_count = member
            column_tiles = per_column[slab_index, red_index]
            return summed + device_partial(column_tiles, integrals, wanted, slot_table, integral_table, live_count), None

        initial = jnp.zeros((GROUP_OUT, TILE, COLUMNS), jnp.float32)
        summed, _ = lax.scan(add_member, initial, (red_ids, wanted_rows, slot_group, integral_group, live_group))
        return summed

    sums = lax.map(one_group, (slab_ids, request_rows, slot_rows, integral_ids, live_rows))
    residual = sums.reshape(OUT_TOTAL, TILE, COLUMNS)
    return residual / denominators
```

```python
import functools

import jax
import jax.numpy as jnp
from jax import lax
from jax.experimental import pallas as pl
from jax.experimental.pallas import tpu as pltpu
from jax.sharding import PartitionSpec as P

VMEM = pltpu.VMEM
SMEM = pltpu.SMEM
LIFT = 2.0**13
WIDTH = 4


def contract(per_chip, flip, place, live, slots, ints, integrals, pulled, out):
    tiles = out.shape[0]
    slot_count = slots.shape[1]
    half = lax.bitwise_xor(lax.rem(place[0], 2), flip)
    live_count = live[0]
    groups = lax.div(live_count + (WIDTH - 1), WIDTH)

    def tile(t, _):
        q = lax.div(t, per_chip) * (2 * per_chip) + half * per_chip + lax.rem(t, per_chip)

        def some(g):
            left, right = [], []
            for w in range(WIDTH):
                k = jnp.minimum(g * WIDTH + w, slot_count - 1)
                alive = g * WIDTH + w < live_count
                block = integrals[ints[q, k]]
                left.append(jnp.where(alive, block, jnp.zeros_like(block)))
                right.append(pulled[slots[q, k]])
            return jnp.dot(
                jnp.concatenate(left, axis=1),
                jnp.concatenate(right, axis=0),
                preferred_element_type=jnp.float32,
            )

        out[t] = some(0)

        def more(g, _):
            out[t] += some(g)
            return 0

        lax.fori_loop(1, groups, more, 0)
        return 0

    lax.fori_loop(0, tiles, tile, 0)


def call_contract(flip, per_chip, tiles, place, live, slots, ints, integrals, pulled):
    rows, columns = integrals.shape[1], pulled.shape[2]
    return pl.pallas_call(
        functools.partial(contract, per_chip, flip),
        out_shape=jax.ShapeDtypeStruct((tiles, rows, columns), jnp.float32),
        in_specs=[pl.BlockSpec(memory_space=SMEM)] * 4 + [pl.BlockSpec(memory_space=VMEM)] * 2,
        out_specs=pl.BlockSpec(memory_space=VMEM),
        compiler_params=pltpu.CompilerParams(vmem_limit_bytes=32 * 2**20),
        cost_estimate=pl.CostEstimate(
            flops=2 * tiles * 12 * rows * rows * columns,
            bytes_accessed=4 * tiles * rows * columns,
            transcendentals=0,
        ),
    )(place, live, slots, ints, integrals, pulled)


def combine(per_chip, place, mine, came, own, *sends):
    chips = len(sends) + 1
    here = lax.div(place[0], 2)
    for d in range(chips):
        first = lax.rem(here + d, chips) * per_chip
        target = own if d == 0 else sends[d - 1]
        for j in range(per_chip):
            target[j] = mine[first + j] + came[first + j]


def call_combine(per_chip, chips, place, mine, came):
    shape = jax.ShapeDtypeStruct((per_chip, *mine.shape[1:]), jnp.float32)
    return pl.pallas_call(
        functools.partial(combine, per_chip),
        out_shape=(shape,) * chips,
        in_specs=[pl.BlockSpec(memory_space=SMEM)] + [pl.BlockSpec(memory_space=VMEM)] * 2,
        out_specs=(pl.BlockSpec(memory_space=VMEM),) * chips,
        compiler_params=pltpu.CompilerParams(vmem_limit_bytes=32 * 2**20),
    )(place, mine, came)


def on_device(amplitudes, integrals, requests, task_slot, task_integral, live_tasks, denominators):
    owners = lax.axis_size("owner")
    reds = lax.axis_size("red")
    chips = reds // 2
    group_tiles, slot_count = task_slot.shape[3:]
    per_chip = group_tiles // reds
    tiles = group_tiles // 2
    wanted = requests.reshape(owners)
    slots = task_slot.reshape(group_tiles, slot_count)
    ints = task_integral.reshape(group_tiles, slot_count)
    live = live_tasks.reshape(1)
    place = lax.axis_index("red").reshape(1).astype(jnp.int32)

    every_integral = lax.all_gather(integrals, "slab", axis=0, tiled=True)
    lifted = (amplitudes * jnp.asarray(LIFT, amplitudes.dtype)).astype(jnp.float16)
    every = lax.all_gather(lifted, "owner", axis=0, tiled=True)
    every = every.reshape(owners, -1, *every.shape[1:])
    pulled = jnp.where((wanted == 0)[:, None, None], every[:, 0], every[:, 1])
    pulled = (pulled.astype(jnp.float32) * (1 / LIFT)).astype(jnp.bfloat16)

    tables = (place, live, slots, ints, every_integral, pulled)
    other = call_contract(1, per_chip, tiles, *tables)
    came = lax.ppermute(other, "red", [(k, k ^ 1) for k in range(reds)])
    mine = call_contract(0, per_chip, tiles, *tables)
    own, *sends = call_combine(per_chip, chips, place, mine, came)
    total = own
    for d, send in enumerate(sends, 1):
        total = total + lax.ppermute(send, "red", [(k, (k + 2 * d) % reds) for k in range(reds)])
    return total / denominators


def solution(mesh):
    placed = (
        P(("owner", "slab", "red"), None, None),
        P("slab", None, None),
        P("owner", "slab", "red", None),
        P("owner", "slab", "red", None, None),
        P("owner", "slab", "red", None, None),
        P("owner", "slab", "red"),
        P(("owner", "slab", "red"), None, None),
    )
    return jax.shard_map(
        on_device,
        mesh=mesh,
        in_specs=placed,
        out_specs=P(("owner", "slab", "red"), None, None),
        check_vma=False,
    )
```

```python
import functools

import jax
import jax.numpy as jnp
from jax import lax
from jax.experimental import pallas as pl
from jax.experimental.pallas import tpu as pltpu
from jax.sharding import PartitionSpec as P

VMEM = pltpu.VMEM
SMEM = pltpu.SMEM
LIFT = 2.0**13
WIDTH = 4


def place_here():
    return lax.axis_index("red").astype(jnp.int32)


def contract(per_chip, flip, live, slots, ints, integrals, pulled, out):
    tiles = out.shape[0]
    slot_count = slots.shape[2]
    live_count = live[0, 0, 0]
    half = lax.bitwise_xor(lax.rem(place_here(), 2), flip)
    groups = lax.div(live_count + (WIDTH - 1), WIDTH)

    def tile(t, _):
        q = lax.div(t, per_chip) * (2 * per_chip) + half * per_chip + lax.rem(t, per_chip)

        def some(g):
            left, right = [], []
            for w in range(WIDTH):
                k = jnp.minimum(g * WIDTH + w, slot_count - 1)
                alive = g * WIDTH + w < live_count
                block = integrals[ints[0, 0, k, 0, q]]
                left.append(jnp.where(alive, block, jnp.zeros_like(block)))
                right.append(pulled[slots[0, 0, k, 0, q]])
            return jnp.dot(
                jnp.concatenate(left, axis=1),
                jnp.concatenate(right, axis=0),
                preferred_element_type=jnp.float32,
            )

        out[t] = some(0)

        def more(g, _):
            out[t] += some(g)
            return 0

        lax.fori_loop(1, groups, more, 0)
        return 0

    lax.fori_loop(0, tiles, tile, 0)


def call_contract(flip, per_chip, tiles, live, slots, ints, integrals, pulled):
    rows, columns = integrals.shape[1], pulled.shape[2]
    return pl.pallas_call(
        functools.partial(contract, per_chip, flip),
        out_shape=jax.ShapeDtypeStruct((tiles, rows, columns), jnp.float32),
        in_specs=[pl.BlockSpec(memory_space=SMEM)] * 3 + [pl.BlockSpec(memory_space=VMEM)] * 2,
        out_specs=pl.BlockSpec(memory_space=VMEM),
        compiler_params=pltpu.CompilerParams(vmem_limit_bytes=32 * 2**20),
        cost_estimate=pl.CostEstimate(
            flops=2 * tiles * 12 * rows * rows * columns,
            bytes_accessed=4 * tiles * rows * columns,
            transcendentals=0,
        ),
    )(live, slots, ints, integrals, pulled)


def partner(chip, core, step):
    return chip ^ 1 if (core + step) % 2 == 0 else 3 - chip


def combine(per_chip, mine, came, keep, send):
    place = place_here()
    here, core = lax.div(place, 2), lax.rem(place, 2)
    near = lax.bitwise_xor(here, 1)
    first = jnp.where(core == 0, near, 3 - here)
    second = jnp.where(core == 0, 3 - here, near)
    across = lax.bitwise_xor(here, 2)
    for block, target, at in ((first, send, 0), (across, send, 1), (here, keep, 0), (second, keep, 1)):
        for j in range(per_chip):
            t = block * per_chip + j
            target[at, j] = mine[t] + came[t]


def call_combine(per_chip, mine, came):
    shape = jax.ShapeDtypeStruct((2, per_chip, *mine.shape[1:]), jnp.float32)
    return pl.pallas_call(
        functools.partial(combine, per_chip),
        out_shape=(shape, shape),
        in_specs=[pl.BlockSpec(memory_space=VMEM)] * 2,
        out_specs=(pl.BlockSpec(memory_space=VMEM),) * 2,
        compiler_params=pltpu.CompilerParams(vmem_limit_bytes=32 * 2**20),
    )(mine, came)


def on_device(amplitudes, integrals, requests, task_slot, task_integral, live_tasks, denominators):
    owners = lax.axis_size("owner")
    reds = lax.axis_size("red")
    group_tiles = task_slot.shape[3]
    per_chip = group_tiles // reds
    tiles = group_tiles // 2
    wanted = requests.reshape(owners)
    slots, ints = (jnp.transpose(t, (0, 1, 4, 2, 3)) for t in (task_slot, task_integral))

    every_integral = lax.all_gather(integrals, "slab", axis=0, tiled=True)
    lifted = (amplitudes * jnp.asarray(LIFT, amplitudes.dtype)).astype(jnp.float16)
    every = lax.all_gather(lifted, "owner", axis=0, tiled=True)
    every = every.reshape(owners, -1, *every.shape[1:])
    pulled = jnp.where((wanted == 0)[:, None, None], every[:, 0], every[:, 1])
    pulled = (pulled.astype(jnp.float32) * (1 / LIFT)).astype(jnp.bfloat16)

    tables = (live_tasks, slots, ints, every_integral, pulled)
    other = call_contract(1, per_chip, tiles, *tables)
    came = lax.ppermute(other, "red", [(k, k ^ 1) for k in range(reds)])
    mine = call_contract(0, per_chip, tiles, *tables)
    keep, send = call_combine(per_chip, mine, came)
    ways = [[(k, 2 * partner(k // 2, k % 2, step) + k % 2) for k in range(reds)] for step in range(2)]
    half = lax.ppermute(send, "red", ways[0])
    last = lax.ppermute(keep[1] + half[1], "red", ways[1])
    return (keep[0] + half[0] + last) / denominators


def solution(mesh):
    placed = (
        P(("owner", "slab", "red"), None, None),
        P("slab", None, None),
        P("owner", "slab", "red", None),
        P("owner", "slab", "red", None, None),
        P("owner", "slab", "red", None, None),
        P("owner", "slab", "red"),
        P(("owner", "slab", "red"), None, None),
    )
    return jax.shard_map(
        on_device,
        mesh=mesh,
        in_specs=placed,
        out_specs=P(("owner", "slab", "red"), None, None),
        check_vma=False,
    )
```

```python
import functools

import jax
import jax.numpy as jnp
from jax import lax
from jax.experimental import pallas as pl
from jax.experimental.pallas import tpu as pltpu
from jax.sharding import PartitionSpec as P

VMEM = pltpu.VMEM
SMEM = pltpu.SMEM
LIFT = 2.0**13
WIDTH = 4
UNROLL = 2


def place_here():
    return lax.axis_index("red").astype(jnp.int32)


def contract(per_chip, flip, live, slots, ints, near, far, pulled, out):
    tiles = out.shape[0]
    slot_count = slots.shape[2]
    owned = near.shape[0] // 2
    slab, slabs = lax.axis_index("slab").astype(jnp.int32), lax.axis_size("slab")
    core = lax.rem(place_here(), 2)
    live_count = live[0, 0, 0]
    half = lax.bitwise_xor(core, flip)
    sign = 1 - 2 * core

    def integral(index):
        ahead = lax.bitwise_and(sign * (lax.div(index, owned) - slab), slabs - 1)
        inside = lax.rem(index, owned)
        at_near = jnp.where(ahead == slabs - 1, owned, 0) + inside
        at_far = jnp.where(ahead == 2, owned, 0) + inside
        is_near = jnp.logical_or(ahead == 0, ahead == slabs - 1)
        return jnp.where(is_near, near[at_near], far[at_far])

    def product(q, groups):
        left, right = [], []
        for k in range(groups * WIDTH):
            block = integral(ints[0, 0, k, 0, q])
            if k >= (groups - 1) * WIDTH:
                block = jnp.where(k < live_count, block, jnp.zeros_like(block))
            left.append(block)
            right.append(pulled[slots[0, 0, k, 0, q]])
        return jnp.dot(
            jnp.concatenate(left, axis=1), jnp.concatenate(right, axis=0), preferred_element_type=jnp.float32
        )

    for groups in range(1, slot_count // WIDTH + 1):

        @pl.when(lax.div(live_count + (WIDTH - 1), WIDTH) == groups)
        def _(groups=groups):
            def tile(t, _):
                q = lax.div(t, per_chip) * (2 * per_chip) + half * per_chip + lax.rem(t, per_chip)
                out[t] = product(q, groups)
                return 0

            lax.fori_loop(0, tiles, tile, 0, unroll=UNROLL)


def call_contract(flip, per_chip, tiles, live, slots, ints, near, far, pulled):
    rows, columns = near.shape[1], pulled.shape[2]
    return pl.pallas_call(
        functools.partial(contract, per_chip, flip),
        out_shape=jax.ShapeDtypeStruct((tiles, rows, columns), jnp.float32),
        in_specs=[pl.BlockSpec(memory_space=SMEM)] * 3 + [pl.BlockSpec(memory_space=VMEM)] * 3,
        out_specs=pl.BlockSpec(memory_space=VMEM),
        compiler_params=pltpu.CompilerParams(vmem_limit_bytes=32 * 2**20),
        cost_estimate=pl.CostEstimate(
            flops=2 * tiles * 12 * rows * rows * columns,
            bytes_accessed=4 * tiles * rows * columns,
            transcendentals=0,
        ),
    )(live, slots, ints, near, far, pulled)


def partner(chip, core, step):
    return chip ^ 1 if (core + step) % 2 == 0 else 3 - chip


def combine(per_chip, mine, came, keep, send):
    place = place_here()
    here, core = lax.div(place, 2), lax.rem(place, 2)
    near = lax.bitwise_xor(here, 1)
    first = jnp.where(core == 0, near, 3 - here)
    second = jnp.where(core == 0, 3 - here, near)
    across = lax.bitwise_xor(here, 2)
    for block, target, at in ((first, send, 0), (across, send, 1), (here, keep, 0), (second, keep, 1)):
        for j in range(per_chip):
            t = block * per_chip + j
            target[at, j] = mine[t] + came[t]


def call_combine(per_chip, mine, came):
    shape = jax.ShapeDtypeStruct((2, per_chip, *mine.shape[1:]), jnp.float32)
    return pl.pallas_call(
        functools.partial(combine, per_chip),
        out_shape=(shape, shape),
        in_specs=[pl.BlockSpec(memory_space=VMEM)] * 2,
        out_specs=(pl.BlockSpec(memory_space=VMEM),) * 2,
        compiler_params=pltpu.CompilerParams(vmem_limit_bytes=32 * 2**20),
    )(mine, came)


def on_device(amplitudes, integrals, requests, task_slot, task_integral, live_tasks, denominators):
    owners = lax.axis_size("owner")
    reds = lax.axis_size("red")
    group_tiles = task_slot.shape[3]
    per_chip = group_tiles // reds
    tiles = group_tiles // 2
    wanted = requests.reshape(owners)
    slots, ints = (jnp.transpose(t, (0, 1, 4, 2, 3)) for t in (task_slot, task_integral))

    slabs = lax.axis_size("slab")
    both = ("slab", "red")

    def at(slab, red):
        return (slab % slabs) * reds + red

    up = [(k, 1 - 2 * (k % 2)) for k in range(reds)]
    one = [(at(s, k), at(s + d, k)) for s in range(slabs) for k, d in up]
    two = [(at(s, k), at(s + d, k ^ 1)) for s in range(slabs) for k, d in up]
    behind = lax.ppermute(integrals, both, one)
    near = jnp.concatenate([integrals, behind], axis=0)
    far = lax.ppermute(near, both, two)
    lifted = (amplitudes * jnp.asarray(LIFT, amplitudes.dtype)).astype(jnp.float16)
    every = lax.all_gather(lifted, "owner", axis=0, tiled=True)
    every = every.reshape(owners, -1, *every.shape[1:])
    pulled = jnp.where((wanted == 0)[:, None, None], every[:, 0], every[:, 1])
    pulled = (pulled.astype(jnp.float32) * (1 / LIFT)).astype(jnp.bfloat16)

    tables = (live_tasks, slots, ints, near, far, pulled)
    other = call_contract(1, per_chip, tiles, *tables)
    came = lax.ppermute(other, "red", [(k, k ^ 1) for k in range(reds)])
    mine = call_contract(0, per_chip, tiles, *tables)
    keep, send = call_combine(per_chip, mine, came)
    ways = [[(k, 2 * partner(k // 2, k % 2, step) + k % 2) for k in range(reds)] for step in range(2)]
    half = lax.ppermute(send, "red", ways[0])
    last = lax.ppermute(keep[1] + half[1], "red", ways[1])
    return (keep[0] + half[0] + last) / denominators


def solution(mesh):
    placed = (
        P(("owner", "slab", "red"), None, None),
        P("slab", None, None),
        P("owner", "slab", "red", None),
        P("owner", "slab", "red", None, None),
        P("owner", "slab", "red", None, None),
        P("owner", "slab", "red"),
        P(("owner", "slab", "red"), None, None),
    )
    return jax.shard_map(
        on_device,
        mesh=mesh,
        in_specs=placed,
        out_specs=P(("owner", "slab", "red"), None, None),
        check_vma=False,
    )
```

```python
import functools

import jax
import jax.numpy as jnp
from jax import lax
from jax.experimental import pallas as pl
from jax.experimental.pallas import tpu as pltpu
from jax.sharding import PartitionSpec as P

VMEM = pltpu.VMEM
SMEM = pltpu.SMEM
LIFT = 2.0**13
WIDTH = 4
UNROLL = 2


def place_here():
    return lax.axis_index("red").astype(jnp.int32)


def contract(per_chip, flip, live, slots, ints, near, far, next_given, far_given, pulled, out):
    tiles = out.shape[0]
    slot_count = slots.shape[2]
    owned = next_given.shape[0]
    slab, slabs = lax.axis_index("slab").astype(jnp.int32), lax.axis_size("slab")
    core = lax.rem(place_here(), 2)
    live_count = live[0, 0, 0]
    half = lax.bitwise_xor(core, flip)

    def integral(index, fetcher):
        ahead = lax.bitwise_and(lax.div(index, owned) - slab, slabs - 1)
        inside = lax.rem(index, owned)
        at_far = jnp.where(ahead == 3, owned, 0) + inside
        if fetcher:
            at_near = jnp.where(ahead == 1, owned, 0) + inside
            return jnp.where(ahead < 2, near[at_near], far[at_far])
        return jnp.where(ahead == 0, near[inside], jnp.where(ahead == 1, next_given[inside], far_given[at_far]))

    def product(q, groups, fetcher):
        left, right = [], []
        for k in range(groups * WIDTH):
            block = integral(ints[0, 0, k, 0, q], fetcher)
            if k >= (groups - 1) * WIDTH:
                block = jnp.where(k < live_count, block, jnp.zeros_like(block))
            left.append(block)
            right.append(pulled[slots[0, 0, k, 0, q]])
        return jnp.dot(
            jnp.concatenate(left, axis=1), jnp.concatenate(right, axis=0), preferred_element_type=jnp.float32
        )

    live_groups = lax.div(live_count + (WIDTH - 1), WIDTH)
    for groups in range(1, slot_count // WIDTH + 1):
        for fetcher in (0, 1):

            @pl.when(jnp.logical_and(live_groups == groups, core == fetcher))
            def _(groups=groups, fetcher=fetcher):
                def tile(t, _):
                    q = lax.div(t, per_chip) * (2 * per_chip) + half * per_chip + lax.rem(t, per_chip)
                    out[t] = product(q, groups, fetcher)
                    return 0

                lax.fori_loop(0, tiles, tile, 0, unroll=UNROLL)


def call_contract(flip, per_chip, tiles, live, slots, ints, *blocks):
    rows, columns = blocks[0].shape[1], blocks[-1].shape[2]
    return pl.pallas_call(
        functools.partial(contract, per_chip, flip),
        out_shape=jax.ShapeDtypeStruct((tiles, rows, columns), jnp.float32),
        in_specs=[pl.BlockSpec(memory_space=SMEM)] * 3 + [pl.BlockSpec(memory_space=VMEM)] * len(blocks),
        out_specs=pl.BlockSpec(memory_space=VMEM),
        compiler_params=pltpu.CompilerParams(vmem_limit_bytes=32 * 2**20),
        cost_estimate=pl.CostEstimate(
            flops=2 * tiles * 12 * rows * rows * columns,
            bytes_accessed=4 * tiles * rows * columns,
            transcendentals=0,
        ),
    )(live, slots, ints, *blocks)


def partner(chip, core, step):
    return chip ^ 1 if (core + step) % 2 == 0 else 3 - chip


def combine(per_chip, mine, came, keep, send):
    place = place_here()
    here, core = lax.div(place, 2), lax.rem(place, 2)
    near = lax.bitwise_xor(here, 1)
    first = jnp.where(core == 0, near, 3 - here)
    second = jnp.where(core == 0, 3 - here, near)
    across = lax.bitwise_xor(here, 2)
    for block, target, at in ((first, send, 0), (across, send, 1), (here, keep, 0), (second, keep, 1)):
        for j in range(per_chip):
            t = block * per_chip + j
            target[at, j] = mine[t] + came[t]


def call_combine(per_chip, mine, came):
    shape = jax.ShapeDtypeStruct((2, per_chip, *mine.shape[1:]), jnp.float32)
    return pl.pallas_call(
        functools.partial(combine, per_chip),
        out_shape=(shape, shape),
        in_specs=[pl.BlockSpec(memory_space=VMEM)] * 2,
        out_specs=(pl.BlockSpec(memory_space=VMEM),) * 2,
        compiler_params=pltpu.CompilerParams(vmem_limit_bytes=32 * 2**20),
    )(mine, came)


def on_device(amplitudes, integrals, requests, task_slot, task_integral, live_tasks, denominators):
    owners = lax.axis_size("owner")
    reds = lax.axis_size("red")
    group_tiles = task_slot.shape[3]
    per_chip = group_tiles // reds
    tiles = group_tiles // 2
    wanted = requests.reshape(owners)
    slots, ints = (jnp.transpose(t, (0, 1, 4, 2, 3)) for t in (task_slot, task_integral))

    slabs = lax.axis_size("slab")
    both = ("slab", "red")

    def at(slab, red):
        return (slab % slabs) * reds + red

    fetchers = range(1, reds, 2)
    one = [(at(s + 1, k), at(s, k)) for s in range(slabs) for k in fetchers]
    two = [(at(s + 2, k), at(s, k)) for s in range(slabs) for k in fetchers]
    give = [(k, k ^ 1) for k in fetchers]
    beyond = lax.ppermute(integrals, both, one)
    near = jnp.concatenate([integrals, beyond], axis=0)
    far = lax.ppermute(near, both, two)
    next_given = lax.ppermute(beyond, "red", give)
    lifted = (amplitudes * jnp.asarray(LIFT, amplitudes.dtype)).astype(jnp.float16)
    every = lax.all_gather(lifted, "owner", axis=0, tiled=True)
    every, far = lax.optimization_barrier((every, far))
    far_given = lax.ppermute(far, "red", give)
    every = every.reshape(owners, -1, *every.shape[1:])
    pulled = jnp.where((wanted == 0)[:, None, None], every[:, 0], every[:, 1])
    pulled = (pulled.astype(jnp.float32) * (1 / LIFT)).astype(jnp.bfloat16)

    tables = (live_tasks, slots, ints, near, far, next_given, far_given, pulled)
    other = call_contract(1, per_chip, tiles, *tables)
    came = lax.ppermute(other, "red", [(k, k ^ 1) for k in range(reds)])
    mine = call_contract(0, per_chip, tiles, *tables)
    keep, send = call_combine(per_chip, mine, came)
    ways = [[(k, 2 * partner(k // 2, k % 2, step) + k % 2) for k in range(reds)] for step in range(2)]
    half = lax.ppermute(send, "red", ways[0])
    last = lax.ppermute(keep[1] + half[1], "red", ways[1])
    return (keep[0] + half[0] + last) / denominators


def solution(mesh):
    placed = (
        P(("owner", "slab", "red"), None, None),
        P("slab", None, None),
        P("owner", "slab", "red", None),
        P("owner", "slab", "red", None, None),
        P("owner", "slab", "red", None, None),
        P("owner", "slab", "red"),
        P(("owner", "slab", "red"), None, None),
    )
    return jax.shard_map(
        on_device,
        mesh=mesh,
        in_specs=placed,
        out_specs=P(("owner", "slab", "red"), None, None),
        check_vma=False,
    )
```

```python
import functools

import jax
import jax.numpy as jnp
from jax import lax
from jax.experimental import pallas as pl
from jax.experimental.pallas import tpu as pltpu
from jax.sharding import PartitionSpec as P

VMEM = pltpu.VMEM
SMEM = pltpu.SMEM
LIFT = 2.0**13
WIDTH = 4
UNROLL = 2
TOP = 32760.0
EXTRA = 16


def place_here():
    return lax.axis_index("red").astype(jnp.int32)


def contract(per_chip, flip, live, slots, ints, near, far, next_given, far_given, pulled, out):
    tiles = out.shape[0]
    slot_count = slots.shape[2]
    owned = next_given.shape[0]
    slab, slabs = lax.axis_index("slab").astype(jnp.int32), lax.axis_size("slab")
    core = lax.rem(place_here(), 2)
    live_count = live[0, 0, 0]
    half = lax.bitwise_xor(core, flip)

    def integral(index, fetcher):
        ahead = lax.bitwise_and(lax.div(index, owned) - slab, slabs - 1)
        inside = lax.rem(index, owned)
        at_far = jnp.where(ahead == 3, owned, 0) + inside
        if fetcher:
            at_near = jnp.where(ahead == 1, owned, 0) + inside
            return jnp.where(ahead < 2, near[at_near], far[at_far])
        return jnp.where(ahead == 0, near[inside], jnp.where(ahead == 1, next_given[inside], far_given[at_far]))

    def product(q, groups, fetcher):
        left, right = [], []
        for k in range(groups * WIDTH):
            block = integral(ints[0, 0, k, 0, q], fetcher)
            if k >= (groups - 1) * WIDTH:
                block = jnp.where(k < live_count, block, jnp.zeros_like(block))
            left.append(block)
            right.append(pulled[slots[0, 0, k, 0, q]])
        return jnp.dot(
            jnp.concatenate(left, axis=1), jnp.concatenate(right, axis=0), preferred_element_type=jnp.float32
        )

    live_groups = lax.div(live_count + (WIDTH - 1), WIDTH)
    for groups in range(1, slot_count // WIDTH + 1):
        for fetcher in (0, 1):

            @pl.when(jnp.logical_and(live_groups == groups, core == fetcher))
            def _(groups=groups, fetcher=fetcher):
                def tile(t, _):
                    q = lax.div(t, per_chip) * (2 * per_chip) + half * per_chip + lax.rem(t, per_chip)
                    out[t] = product(q, groups, fetcher)
                    return 0

                lax.fori_loop(0, tiles, tile, 0, unroll=UNROLL)


def call_contract(flip, per_chip, tiles, live, slots, ints, *blocks):
    rows, columns = blocks[0].shape[1], blocks[-1].shape[2]
    return pl.pallas_call(
        functools.partial(contract, per_chip, flip),
        out_shape=jax.ShapeDtypeStruct((tiles, rows, columns), jnp.float32),
        in_specs=[pl.BlockSpec(memory_space=SMEM)] * 3 + [pl.BlockSpec(memory_space=VMEM)] * len(blocks),
        out_specs=pl.BlockSpec(memory_space=VMEM),
        compiler_params=pltpu.CompilerParams(vmem_limit_bytes=32 * 2**20),
        cost_estimate=pl.CostEstimate(
            flops=2 * tiles * 12 * rows * rows * columns,
            bytes_accessed=4 * tiles * rows * columns,
            transcendentals=0,
        ),
    )(live, slots, ints, *blocks)


def partner(chip, core, step):
    return chip ^ 1 if (core + step) % 2 == 0 else 3 - chip


def encode(values, target):
    rows, columns = values.shape
    peak = jnp.maximum(jnp.max(jnp.abs(values), axis=0, keepdims=True), 1e-30)
    exponent = jnp.floor(jnp.log2(peak)) + 1.0
    scaled = values * (jnp.exp2(-exponent) * TOP)
    target[:rows] = jnp.floor(scaled + 0.5).astype(jnp.int32).astype(jnp.int16)
    target[rows:] = jnp.broadcast_to(exponent, (EXTRA, columns)).astype(jnp.int32).astype(jnp.int16)


def decode(source):
    rows = source.shape[0] - EXTRA
    exponent = source[rows:].astype(jnp.int32).astype(jnp.float32)[:1]
    return source[:rows].astype(jnp.int32).astype(jnp.float32) * (jnp.exp2(exponent) * (1 / TOP))


def combine(per_chip, mine, came, keep, send):
    place = place_here()
    here, core = lax.div(place, 2), lax.rem(place, 2)
    near = lax.bitwise_xor(here, 1)
    first = jnp.where(core == 0, near, 3 - here)
    second = jnp.where(core == 0, 3 - here, near)
    across = lax.bitwise_xor(here, 2)
    for at, block in enumerate((first, across)):
        for j in range(per_chip):
            t = block * per_chip + j
            encode(mine[t] + came[t], send.at[at, j])
    for at, block in enumerate((here, second)):
        for j in range(per_chip):
            t = block * per_chip + j
            keep[at, j] = mine[t] + came[t]


def pass_on(keep, half, send):
    for j in range(keep.shape[1]):
        encode(keep[1, j] + decode(half.at[1, j]), send.at[j])


def finish(keep, half, last, denominators, out):
    for j in range(keep.shape[1]):
        out[j] = (keep[0, j] + decode(half.at[0, j]) + decode(last.at[j])) / denominators[j]


def on_chip(kernel, shapes, *arrays):
    return pl.pallas_call(
        kernel,
        out_shape=shapes,
        in_specs=[pl.BlockSpec(memory_space=VMEM)] * len(arrays),
        out_specs=jax.tree.map(lambda _: pl.BlockSpec(memory_space=VMEM), shapes),
        compiler_params=pltpu.CompilerParams(vmem_limit_bytes=32 * 2**20),
    )(*arrays)


def on_device(amplitudes, integrals, requests, task_slot, task_integral, live_tasks, denominators):
    owners = lax.axis_size("owner")
    reds = lax.axis_size("red")
    group_tiles = task_slot.shape[3]
    per_chip = group_tiles // reds
    tiles = group_tiles // 2
    wanted = requests.reshape(owners)
    slots, ints = (jnp.transpose(t, (0, 1, 4, 2, 3)) for t in (task_slot, task_integral))

    slabs = lax.axis_size("slab")
    both = ("slab", "red")

    def at(slab, red):
        return (slab % slabs) * reds + red

    fetchers = range(1, reds, 2)
    one = [(at(s + 1, k), at(s, k)) for s in range(slabs) for k in fetchers]
    two = [(at(s + 2, k), at(s, k)) for s in range(slabs) for k in fetchers]
    give = [(k, k ^ 1) for k in fetchers]
    beyond = lax.ppermute(integrals, both, one)
    near = jnp.concatenate([integrals, beyond], axis=0)
    far = lax.ppermute(near, both, two)
    next_given = lax.ppermute(beyond, "red", give)
    lifted = (amplitudes * jnp.asarray(LIFT, amplitudes.dtype)).astype(jnp.float16)
    every = lax.all_gather(lifted, "owner", axis=0, tiled=True)
    every, far = lax.optimization_barrier((every, far))
    far_given = lax.ppermute(far, "red", give)
    every = every.reshape(owners, -1, *every.shape[1:])
    pulled = jnp.where((wanted == 0)[:, None, None], every[:, 0], every[:, 1])
    pulled = (pulled.astype(jnp.float32) * (1 / LIFT)).astype(jnp.bfloat16)

    tables = (live_tasks, slots, ints, near, far, next_given, far_given, pulled)
    other = call_contract(1, per_chip, tiles, *tables)
    came = lax.ppermute(other, "red", [(k, k ^ 1) for k in range(reds)])
    mine = call_contract(0, per_chip, tiles, *tables)
    rows, columns = mine.shape[1:]
    whole = jax.ShapeDtypeStruct((2, per_chip, rows, columns), jnp.float32)
    coded = jax.ShapeDtypeStruct((2, per_chip, rows + EXTRA, columns), jnp.int16)
    one_coded = jax.ShapeDtypeStruct(coded.shape[1:], jnp.int16)
    keep, send = on_chip(functools.partial(combine, per_chip), (whole, coded), mine, came)
    ways = [[(k, 2 * partner(k // 2, k % 2, step) + k % 2) for k in range(reds)] for step in range(2)]
    half = lax.ppermute(send, "red", ways[0])
    last = lax.ppermute(on_chip(pass_on, one_coded, keep, half), "red", ways[1])
    return on_chip(
        finish, jax.ShapeDtypeStruct(denominators.shape, jnp.float32), keep, half, last, denominators
    )


def solution(mesh):
    placed = (
        P(("owner", "slab", "red"), None, None),
        P("slab", None, None),
        P("owner", "slab", "red", None),
        P("owner", "slab", "red", None, None),
        P("owner", "slab", "red", None, None),
        P("owner", "slab", "red"),
        P(("owner", "slab", "red"), None, None),
    )
    return jax.shard_map(
        on_device,
        mesh=mesh,
        in_specs=placed,
        out_specs=P(("owner", "slab", "red"), None, None),
        check_vma=False,
    )
```

```python
import functools

import jax
import jax.numpy as jnp
from jax import lax
from jax.experimental import pallas as pl
from jax.experimental.pallas import tpu as pltpu
from jax.sharding import PartitionSpec as P

VMEM = pltpu.VMEM
SMEM = pltpu.SMEM
LIFT = 2.0**13
WIDTH = 4
UNROLL = 2
TOP = 32760.0
EXTRA = 16
ORDER = ((2, 1, 3), (2, 3, 1))


def place_here():
    return lax.axis_index("red").astype(jnp.int32)


def contract(per_chip, flip, live, slots, ints, near, far, next_given, far_given, pulled, out):
    tiles = out.shape[0]
    slot_count = slots.shape[2]
    owned = next_given.shape[0]
    slab, slabs = lax.axis_index("slab").astype(jnp.int32), lax.axis_size("slab")
    core = lax.rem(place_here(), 2)
    live_count = live[0, 0, 0]
    half = lax.bitwise_xor(core, flip)

    def integral(index, fetcher):
        ahead = lax.bitwise_and(lax.div(index, owned) - slab, slabs - 1)
        inside = lax.rem(index, owned)
        at_far = jnp.where(ahead == 3, owned, 0) + inside
        if fetcher:
            at_near = jnp.where(ahead == 1, owned, 0) + inside
            return jnp.where(ahead < 2, near[at_near], far[at_far])
        return jnp.where(ahead == 0, near[inside], jnp.where(ahead == 1, next_given[inside], far_given[at_far]))

    def product(q, groups, fetcher):
        left, right = [], []
        for k in range(groups * WIDTH):
            block = integral(ints[0, 0, k, 0, q], fetcher)
            if k >= (groups - 1) * WIDTH:
                block = jnp.where(k < live_count, block, jnp.zeros_like(block))
            left.append(block)
            right.append(pulled[slots[0, 0, k, 0, q]])
        return jnp.dot(
            jnp.concatenate(left, axis=1), jnp.concatenate(right, axis=0), preferred_element_type=jnp.float32
        )

    live_groups = lax.div(live_count + (WIDTH - 1), WIDTH)
    for groups in range(1, slot_count // WIDTH + 1):
        for fetcher in (0, 1):

            @pl.when(jnp.logical_and(live_groups == groups, core == fetcher))
            def _(groups=groups, fetcher=fetcher):
                def tile(t, _):
                    q = lax.div(t, per_chip) * (2 * per_chip) + half * per_chip + lax.rem(t, per_chip)
                    out[t] = product(q, groups, fetcher)
                    return 0

                lax.fori_loop(0, tiles, tile, 0, unroll=UNROLL)


def call_contract(flip, per_chip, tiles, live, slots, ints, *blocks):
    rows, columns = blocks[0].shape[1], blocks[-1].shape[2]
    return pl.pallas_call(
        functools.partial(contract, per_chip, flip),
        out_shape=jax.ShapeDtypeStruct((tiles, rows, columns), jnp.float32),
        in_specs=[pl.BlockSpec(memory_space=SMEM)] * 3 + [pl.BlockSpec(memory_space=VMEM)] * len(blocks),
        out_specs=pl.BlockSpec(memory_space=VMEM),
        compiler_params=pltpu.CompilerParams(vmem_limit_bytes=32 * 2**20),
        cost_estimate=pl.CostEstimate(
            flops=2 * tiles * 12 * rows * rows * columns,
            bytes_accessed=4 * tiles * rows * columns,
            transcendentals=0,
        ),
    )(live, slots, ints, *blocks)


def encode(values, target):
    rows, columns = values.shape
    peak = jnp.maximum(jnp.max(jnp.abs(values), axis=0, keepdims=True), 1e-30)
    exponent = jnp.floor(jnp.log2(peak)) + 1.0
    scaled = values * (jnp.exp2(-exponent) * TOP)
    target[:rows] = jnp.floor(scaled + 0.5).astype(jnp.int32).astype(jnp.int16)
    target[rows:] = jnp.broadcast_to(exponent, (EXTRA, columns)).astype(jnp.int32).astype(jnp.int16)


def decode(source):
    rows = source.shape[0] - EXTRA
    exponent = source[rows:].astype(jnp.int32).astype(jnp.float32)[:1]
    return source[:rows].astype(jnp.int32).astype(jnp.float32) * (jnp.exp2(exponent) * (1 / TOP))


def steps_of(core):
    return ORDER[core]


def combine(per_chip, mine, came, keep, *sends):
    place = place_here()
    here, core = lax.div(place, 2), lax.rem(place, 2)
    for send, zero, one in zip(sends, steps_of(0), steps_of(1)):
        block = lax.rem(here + jnp.where(core == 0, zero, one), len(sends) + 1)
        for j in range(per_chip):
            t = block * per_chip + j
            encode(mine[t] + came[t], send.at[j])
    for j in range(per_chip):
        t = here * per_chip + j
        keep[j] = mine[t] + came[t]


def finish(keep, first, second, third, denominators, out):
    for j in range(keep.shape[0]):
        total = keep[j] + decode(first.at[j]) + decode(second.at[j]) + decode(third.at[j])
        out[j] = total / denominators[j]


def on_chip(kernel, shapes, *arrays):
    return pl.pallas_call(
        kernel,
        out_shape=shapes,
        in_specs=[pl.BlockSpec(memory_space=VMEM)] * len(arrays),
        out_specs=jax.tree.map(lambda _: pl.BlockSpec(memory_space=VMEM), shapes),
        compiler_params=pltpu.CompilerParams(vmem_limit_bytes=32 * 2**20),
    )(*arrays)


def on_device(amplitudes, integrals, requests, task_slot, task_integral, live_tasks, denominators):
    owners = lax.axis_size("owner")
    reds = lax.axis_size("red")
    group_tiles = task_slot.shape[3]
    per_chip = group_tiles // reds
    tiles = group_tiles // 2
    wanted = requests.reshape(owners)
    slots, ints = (jnp.transpose(t, (0, 1, 4, 2, 3)) for t in (task_slot, task_integral))

    slabs = lax.axis_size("slab")
    both = ("slab", "red")

    def at(slab, red):
        return (slab % slabs) * reds + red

    fetchers = range(1, reds, 2)
    one = [(at(s + 1, k), at(s, k)) for s in range(slabs) for k in fetchers]
    two = [(at(s + 2, k), at(s, k)) for s in range(slabs) for k in fetchers]
    give = [(k, k ^ 1) for k in fetchers]
    beyond = lax.ppermute(integrals, both, one)
    near = jnp.concatenate([integrals, beyond], axis=0)
    far = lax.ppermute(near, both, two)
    next_given = lax.ppermute(beyond, "red", give)
    lifted = (amplitudes * jnp.asarray(LIFT, amplitudes.dtype)).astype(jnp.float16)
    every = lax.all_gather(lifted, "owner", axis=0, tiled=True)
    every, far = lax.optimization_barrier((every, far))
    far_given = lax.ppermute(far, "red", give)
    every = every.reshape(owners, -1, *every.shape[1:])
    pulled = jnp.where((wanted == 0)[:, None, None], every[:, 0], every[:, 1])
    pulled = (pulled.astype(jnp.float32) * (1 / LIFT)).astype(jnp.bfloat16)

    tables = (live_tasks, slots, ints, near, far, next_given, far_given, pulled)
    other = call_contract(1, per_chip, tiles, *tables)
    came = lax.ppermute(other, "red", [(k, k ^ 1) for k in range(reds)])
    mine = call_contract(0, per_chip, tiles, *tables)
    rows, columns = mine.shape[1:]
    whole = jax.ShapeDtypeStruct((per_chip, rows, columns), jnp.float32)
    coded = jax.ShapeDtypeStruct((per_chip, rows + EXTRA, columns), jnp.int16)
    keep, *sends = on_chip(functools.partial(combine, per_chip), (whole, coded, coded, coded), mine, came)
    parts = [
        lax.ppermute(send, "red", [(k, (k + 2 * steps_of(k % 2)[i]) % reds) for k in range(reds)])
        for i, send in enumerate(sends)
    ]
    return on_chip(
        finish, jax.ShapeDtypeStruct(denominators.shape, jnp.float32), keep, *parts, denominators
    )


def solution(mesh):
    placed = (
        P(("owner", "slab", "red"), None, None),
        P("slab", None, None),
        P("owner", "slab", "red", None),
        P("owner", "slab", "red", None, None),
        P("owner", "slab", "red", None, None),
        P("owner", "slab", "red"),
        P(("owner", "slab", "red"), None, None),
    )
    return jax.shard_map(
        on_device,
        mesh=mesh,
        in_specs=placed,
        out_specs=P(("owner", "slab", "red"), None, None),
        check_vma=False,
    )
```

```python
import functools

import jax
import jax.numpy as jnp
from jax import lax
from jax.experimental import pallas as pl
from jax.experimental.pallas import tpu as pltpu
from jax.sharding import PartitionSpec as P

VMEM = pltpu.VMEM
SMEM = pltpu.SMEM
LIFT = 2.0**13
WIDTH = 4
UNROLL = 4
TOP = 32760.0
EXTRA = 16
ORDER = ((2, 1, 3), (2, 3, 1))


def place_here():
    return lax.axis_index("red").astype(jnp.int32)


def contract(per_chip, flip, live, slots, ints, near, far, next_given, far_given, pulled, out):
    tiles = out.shape[0]
    slot_count = slots.shape[2]
    owned = next_given.shape[0]
    slab, slabs = lax.axis_index("slab").astype(jnp.int32), lax.axis_size("slab")
    core = lax.rem(place_here(), 2)
    live_count = live[0, 0, 0]
    half = lax.bitwise_xor(core, flip)

    def integral(index, fetcher):
        ahead = lax.bitwise_and(lax.div(index, owned) - slab, slabs - 1)
        inside = lax.rem(index, owned)
        at_far = jnp.where(ahead == 3, owned, 0) + inside
        if fetcher:
            at_near = jnp.where(ahead == 1, owned, 0) + inside
            return jnp.where(ahead < 2, near[at_near], far[at_far])
        return jnp.where(ahead == 0, near[inside], jnp.where(ahead == 1, next_given[inside], far_given[at_far]))

    def product(q, groups, fetcher):
        left, right = [], []
        for k in range(groups * WIDTH):
            block = integral(ints[0, 0, k, 0, q], fetcher)
            if k >= (groups - 1) * WIDTH:
                block = jnp.where(k < live_count, block, jnp.zeros_like(block))
            left.append(block)
            right.append(pulled[slots[0, 0, k, 0, q]])
        return jnp.dot(
            jnp.concatenate(left, axis=1), jnp.concatenate(right, axis=0), preferred_element_type=jnp.float32
        )

    live_groups = lax.div(live_count + (WIDTH - 1), WIDTH)
    for groups in range(1, slot_count // WIDTH + 1):
        for fetcher in (0, 1):

            @pl.when(jnp.logical_and(live_groups == groups, core == fetcher))
            def _(groups=groups, fetcher=fetcher):
                def tile(t, _):
                    q = lax.div(t, per_chip) * (2 * per_chip) + half * per_chip + lax.rem(t, per_chip)
                    out[t] = product(q, groups, fetcher)
                    return 0

                lax.fori_loop(0, tiles, tile, 0, unroll=UNROLL)


def call_contract(flip, per_chip, tiles, live, slots, ints, *blocks):
    rows, columns = blocks[0].shape[1], blocks[-1].shape[2]
    return pl.pallas_call(
        functools.partial(contract, per_chip, flip),
        out_shape=jax.ShapeDtypeStruct((tiles, rows, columns), jnp.float32),
        in_specs=[pl.BlockSpec(memory_space=SMEM)] * 3 + [pl.BlockSpec(memory_space=VMEM)] * len(blocks),
        out_specs=pl.BlockSpec(memory_space=VMEM),
        compiler_params=pltpu.CompilerParams(vmem_limit_bytes=32 * 2**20),
        cost_estimate=pl.CostEstimate(
            flops=2 * tiles * 12 * rows * rows * columns,
            bytes_accessed=4 * tiles * rows * columns,
            transcendentals=0,
        ),
    )(live, slots, ints, *blocks)


def encode(values, target):
    rows, columns = values.shape
    peak = jnp.maximum(jnp.max(jnp.abs(values), axis=0, keepdims=True), 1e-30)
    exponent = jnp.floor(jnp.log2(peak)) + 1.0
    scaled = values * (jnp.exp2(-exponent) * TOP)
    target[:rows] = jnp.floor(scaled + 0.5).astype(jnp.int32).astype(jnp.int16)
    target[rows:] = jnp.broadcast_to(exponent, (EXTRA, columns)).astype(jnp.int32).astype(jnp.int16)


def decode(source):
    rows = source.shape[0] - EXTRA
    exponent = source[rows:].astype(jnp.int32).astype(jnp.float32)[:1]
    return source[:rows].astype(jnp.int32).astype(jnp.float32) * (jnp.exp2(exponent) * (1 / TOP))


def steps_of(core):
    return ORDER[core]


def combine(per_chip, mine, came, keep, *sends):
    place = place_here()
    here, core = lax.div(place, 2), lax.rem(place, 2)
    for send, zero, one in zip(sends, steps_of(0), steps_of(1)):
        block = lax.rem(here + jnp.where(core == 0, zero, one), len(sends) + 1)
        for j in range(per_chip):
            t = block * per_chip + j
            encode(mine[t] + came[t], send.at[j])
    for j in range(per_chip):
        t = here * per_chip + j
        keep[j] = mine[t] + came[t]


def finish(keep, first, second, third, denominators, out):
    for j in range(keep.shape[0]):
        total = keep[j] + decode(first.at[j]) + decode(second.at[j]) + decode(third.at[j])
        out[j] = total / denominators[j]


def on_chip(kernel, shapes, *arrays):
    return pl.pallas_call(
        kernel,
        out_shape=shapes,
        in_specs=[pl.BlockSpec(memory_space=VMEM)] * len(arrays),
        out_specs=jax.tree.map(lambda _: pl.BlockSpec(memory_space=VMEM), shapes),
        compiler_params=pltpu.CompilerParams(vmem_limit_bytes=32 * 2**20),
    )(*arrays)


def on_device(amplitudes, integrals, requests, task_slot, task_integral, live_tasks, denominators):
    owners = lax.axis_size("owner")
    reds = lax.axis_size("red")
    group_tiles = task_slot.shape[3]
    per_chip = group_tiles // reds
    tiles = group_tiles // 2
    wanted = requests.reshape(owners)
    slots, ints = (jnp.transpose(t, (0, 1, 4, 2, 3)) for t in (task_slot, task_integral))

    slabs = lax.axis_size("slab")
    both = ("slab", "red")

    def at(slab, red):
        return (slab % slabs) * reds + red

    fetchers = range(1, reds, 2)
    one = [(at(s + 1, k), at(s, k)) for s in range(slabs) for k in fetchers]
    two = [(at(s + 2, k), at(s, k)) for s in range(slabs) for k in fetchers]
    give = [(k, k ^ 1) for k in fetchers]
    beyond = lax.ppermute(integrals, both, one)
    near = jnp.concatenate([integrals, beyond], axis=0)
    far = lax.ppermute(near, both, two)
    next_given = lax.ppermute(beyond, "red", give)
    lifted = (amplitudes * jnp.asarray(LIFT, amplitudes.dtype)).astype(jnp.float16)
    every = lax.all_gather(lifted, "owner", axis=0, tiled=True)
    every, far, next_given = lax.optimization_barrier((every, far, next_given))
    far_given = lax.ppermute(far, "red", give)
    every = every.reshape(owners, -1, *every.shape[1:])
    pulled = jnp.where((wanted == 0)[:, None, None], every[:, 0], every[:, 1])
    pulled = (pulled.astype(jnp.float32) * (1 / LIFT)).astype(jnp.bfloat16)

    tables = (live_tasks, slots, ints, near, far, next_given, far_given, pulled)
    other = call_contract(1, per_chip, tiles, *tables)
    came = lax.ppermute(other, "red", [(k, k ^ 1) for k in range(reds)])
    mine = call_contract(0, per_chip, tiles, *tables)
    rows, columns = mine.shape[1:]
    whole = jax.ShapeDtypeStruct((per_chip, rows, columns), jnp.float32)
    coded = jax.ShapeDtypeStruct((per_chip, rows + EXTRA, columns), jnp.int16)
    keep, *sends = on_chip(functools.partial(combine, per_chip), (whole, coded, coded, coded), mine, came)
    parts = [
        lax.ppermute(send, "red", [(k, (k + 2 * steps_of(k % 2)[i]) % reds) for k in range(reds)])
        for i, send in enumerate(sends)
    ]
    return on_chip(
        finish, jax.ShapeDtypeStruct(denominators.shape, jnp.float32), keep, *parts, denominators
    )


def solution(mesh):
    placed = (
        P(("owner", "slab", "red"), None, None),
        P("slab", None, None),
        P("owner", "slab", "red", None),
        P("owner", "slab", "red", None, None),
        P("owner", "slab", "red", None, None),
        P("owner", "slab", "red"),
        P(("owner", "slab", "red"), None, None),
    )
    return jax.shard_map(
        on_device,
        mesh=mesh,
        in_specs=placed,
        out_specs=P(("owner", "slab", "red"), None, None),
        check_vma=False,
    )
```

```python
import functools

import jax
import jax.numpy as jnp
from jax import lax
from jax.experimental import pallas as pl
from jax.experimental.pallas import tpu as pltpu
from jax.sharding import PartitionSpec as P

VMEM = pltpu.VMEM
SMEM = pltpu.SMEM
LIFT = 2.0**13
WIDTH = 4
UNROLL = 8
TOP = 32760.0
EXTRA = 16
ORDER = ((2, 1, 3), (2, 3, 1))


def place_here():
    return lax.axis_index("red").astype(jnp.int32)


def contract(per_chip, flip, live, slots, ints, near, far, next_given, far_given, pulled, out):
    tiles = out.shape[0]
    slot_count = slots.shape[2]
    owned = next_given.shape[0]
    slab, slabs = lax.axis_index("slab").astype(jnp.int32), lax.axis_size("slab")
    core = lax.rem(place_here(), 2)
    live_count = live[0, 0, 0]
    half = lax.bitwise_xor(core, flip)

    def integral(index, fetcher):
        ahead = lax.bitwise_and(lax.div(index, owned) - slab, slabs - 1)
        inside = lax.rem(index, owned)
        at_far = jnp.where(ahead == 3, owned, 0) + inside
        if fetcher:
            at_near = jnp.where(ahead == 1, owned, 0) + inside
            return jnp.where(ahead < 2, near[at_near], far[at_far])
        return jnp.where(ahead == 0, near[inside], jnp.where(ahead == 1, next_given[inside], far_given[at_far]))

    def product(q, groups, fetcher):
        left, right = [], []
        for k in range(groups * WIDTH):
            block = integral(ints[0, 0, k, 0, q], fetcher)
            if k >= (groups - 1) * WIDTH:
                block = jnp.where(k < live_count, block, jnp.zeros_like(block))
            left.append(block)
            right.append(pulled[slots[0, 0, k, 0, q]])
        return jnp.dot(
            jnp.concatenate(left, axis=1), jnp.concatenate(right, axis=0), preferred_element_type=jnp.float32
        )

    live_groups = lax.div(live_count + (WIDTH - 1), WIDTH)
    for groups in range(1, slot_count // WIDTH + 1):
        for fetcher in (0, 1):

            @pl.when(jnp.logical_and(live_groups == groups, core == fetcher))
            def _(groups=groups, fetcher=fetcher):
                def tile(t, _):
                    q = lax.div(t, per_chip) * (2 * per_chip) + half * per_chip + lax.rem(t, per_chip)
                    out[t] = product(q, groups, fetcher)
                    return 0

                lax.fori_loop(0, tiles, tile, 0, unroll=UNROLL)


def call_contract(flip, per_chip, tiles, live, slots, ints, *blocks):
    rows, columns = blocks[0].shape[1], blocks[-1].shape[2]
    return pl.pallas_call(
        functools.partial(contract, per_chip, flip),
        out_shape=jax.ShapeDtypeStruct((tiles, rows, columns), jnp.float32),
        in_specs=[pl.BlockSpec(memory_space=SMEM)] * 3 + [pl.BlockSpec(memory_space=VMEM)] * len(blocks),
        out_specs=pl.BlockSpec(memory_space=VMEM),
        compiler_params=pltpu.CompilerParams(vmem_limit_bytes=32 * 2**20),
        cost_estimate=pl.CostEstimate(
            flops=2 * tiles * 12 * rows * rows * columns,
            bytes_accessed=4 * tiles * rows * columns,
            transcendentals=0,
        ),
    )(live, slots, ints, *blocks)


def encode(values, target):
    rows, columns = values.shape
    peak = jnp.maximum(jnp.max(jnp.abs(values), axis=0, keepdims=True), 1e-30)
    exponent = jnp.floor(jnp.log2(peak)) + 1.0
    scaled = values * (jnp.exp2(-exponent) * TOP)
    target[:rows] = jnp.floor(scaled + 0.5).astype(jnp.int32).astype(jnp.int16)
    target[rows:] = jnp.broadcast_to(exponent, (EXTRA, columns)).astype(jnp.int32).astype(jnp.int16)


def decode(source):
    rows = source.shape[0] - EXTRA
    exponent = source[rows:].astype(jnp.int32).astype(jnp.float32)[:1]
    return source[:rows].astype(jnp.int32).astype(jnp.float32) * (jnp.exp2(exponent) * (1 / TOP))


def steps_of(core):
    return ORDER[core]


def combine(per_chip, mine, came, keep, *sends):
    place = place_here()
    here, core = lax.div(place, 2), lax.rem(place, 2)
    for send, zero, one in zip(sends, steps_of(0), steps_of(1)):
        block = lax.rem(here + jnp.where(core == 0, zero, one), len(sends) + 1)
        for j in range(per_chip):
            t = block * per_chip + j
            encode(mine[t] + came[t], send.at[j])
    for j in range(per_chip):
        t = here * per_chip + j
        keep[j] = mine[t] + came[t]


def finish(keep, first, second, third, denominators, out):
    for j in range(keep.shape[0]):
        total = keep[j] + decode(first.at[j]) + decode(second.at[j]) + decode(third.at[j])
        out[j] = total / denominators[j]


def on_chip(kernel, shapes, *arrays):
    return pl.pallas_call(
        kernel,
        out_shape=shapes,
        in_specs=[pl.BlockSpec(memory_space=VMEM)] * len(arrays),
        out_specs=jax.tree.map(lambda _: pl.BlockSpec(memory_space=VMEM), shapes),
        compiler_params=pltpu.CompilerParams(vmem_limit_bytes=32 * 2**20),
    )(*arrays)


def on_device(amplitudes, integrals, requests, task_slot, task_integral, live_tasks, denominators):
    owners = lax.axis_size("owner")
    reds = lax.axis_size("red")
    group_tiles = task_slot.shape[3]
    per_chip = group_tiles // reds
    tiles = group_tiles // 2
    wanted = requests.reshape(owners)
    slots, ints = (jnp.transpose(t, (0, 1, 4, 2, 3)) for t in (task_slot, task_integral))

    slabs = lax.axis_size("slab")
    both = ("slab", "red")

    def at(slab, red):
        return (slab % slabs) * reds + red

    fetchers = range(1, reds, 2)
    one = [(at(s + 1, k), at(s, k)) for s in range(slabs) for k in fetchers]
    two = [(at(s + 2, k), at(s, k)) for s in range(slabs) for k in fetchers]
    give = [(k, k ^ 1) for k in fetchers]
    beyond = lax.ppermute(integrals, both, one)
    near = jnp.concatenate([integrals, beyond], axis=0)
    far = lax.ppermute(near, both, two)
    next_given = lax.ppermute(beyond, "red", give)
    lifted = (amplitudes * jnp.asarray(LIFT, amplitudes.dtype)).astype(jnp.float16)
    every = lax.all_gather(lifted, "owner", axis=0, tiled=True)
    every, far, next_given = lax.optimization_barrier((every, far, next_given))
    far_given = lax.ppermute(far, "red", give)
    every = every.reshape(owners, -1, *every.shape[1:])
    pulled = jnp.where((wanted == 0)[:, None, None], every[:, 0], every[:, 1])
    pulled = (pulled.astype(jnp.float32) * (1 / LIFT)).astype(jnp.bfloat16)

    tables = (live_tasks, slots, ints, near, far, next_given, far_given, pulled)
    other = call_contract(1, per_chip, tiles, *tables)
    came = lax.ppermute(other, "red", [(k, k ^ 1) for k in range(reds)])
    mine = call_contract(0, per_chip, tiles, *tables)
    rows, columns = mine.shape[1:]
    whole = jax.ShapeDtypeStruct((per_chip, rows, columns), jnp.float32)
    coded = jax.ShapeDtypeStruct((per_chip, rows + EXTRA, columns), jnp.int16)
    keep, *sends = on_chip(functools.partial(combine, per_chip), (whole, coded, coded, coded), mine, came)
    parts = [
        lax.ppermute(send, "red", [(k, (k + 2 * steps_of(k % 2)[i]) % reds) for k in range(reds)])
        for i, send in enumerate(sends)
    ]
    return on_chip(
        finish, jax.ShapeDtypeStruct(denominators.shape, jnp.float32), keep, *parts, denominators
    )


def solution(mesh):
    placed = (
        P(("owner", "slab", "red"), None, None),
        P("slab", None, None),
        P("owner", "slab", "red", None),
        P("owner", "slab", "red", None, None),
        P("owner", "slab", "red", None, None),
        P("owner", "slab", "red"),
        P(("owner", "slab", "red"), None, None),
    )
    return jax.shard_map(
        on_device,
        mesh=mesh,
        in_specs=placed,
        out_specs=P(("owner", "slab", "red"), None, None),
        check_vma=False,
    )
```
